32 devices in a mesh: row: 4 (over x, core), aux: 8 (over z, y).
Axes of the slice: x: 2, y: 2, z: 4, core: 2. Of those that a mesh axis runs over, the one named last changes fastest.
Arguments:
- tiles: bfloat16 [128, 1024, 256], P('aux', 'row'), may hold values from -6 to 6
- block_ids: int32 [4, 8, 2], P('row'), may hold values from 0 to 39, all different within a row
- coeffs: bfloat16 [5120, 256], P('row'), may hold values from -0.375 to 0.375
- energies: float32 [256], replicated, may hold values from -1.5 to -0.2
- tau: float32 [2], replicated, may hold values from 0.2 to 2
- weights: float32 [2], replicated, may hold values from 0.3 to 1.5
- coupling: bfloat16 [128, 128], replicated, may hold values from -0.5 to 0.5
Outputs:
- gamma: bfloat16 [1024, 128, 256], P(('row', 'aux'))
The draws below stay inside these ranges and needn't reach their ends.
Inputs may be any that keep to these rules, and one draw needn't show every extreme that they name: `block_ids`: within one row slab and auxiliary slab the 2 block numbers differ; every block number is kept by some slab.
All inputs are finite; a program needn't handle non-finite values.
Results may differ from the reference program's by a relative error of at most 0.006.
Values may be sent and summed in bfloat16 or wider, within the bound.
No kernel may reach another device: no remote copies, remote signals or barrier semaphores. Data moves between devices by JAX's collectives and lax.ppermute only.
A program may use at most 64 MiB of HBM per device.

```python
import math
import jax
import jax.numpy as jnp
from jax import lax

N = 5120
BLK = 128
NBLK = 40
O = 256
POINTS = 2
NSCR = 2
COLS = 256
ROW_DEV = 256
AUX_DEV = 16
SLABS_ROW = 4
SLABS_AUX = 8
ROWS = 1024
AUX_FNS = 128


def block_scale(own_key, shape, cuts, least, top_value):
    factor_of, own = 1.0, jax.random.fold_in(own_key, 6)
    for position, blocks in cuts:
        steps = jnp.exp(jax.random.uniform(jax.random.fold_in(own, position), (blocks,), jnp.float32, least / len(cuts), top_value / len(cuts)))
        factor_of = factor_of * jnp.repeat(steps, shape[position] // blocks).reshape([-1 if axis == position else 1 for axis in range(len(shape))])
    return factor_of


def different_ones(rng, rows, count, top, lift):
    order = jax.random.permutation(jax.random.fold_in(rng, 1), count)
    boost = order
    for power in range(3):
        boost = boost * boost // count
    boost = boost * lift // count
    tickets = jax.random.randint(jax.random.fold_in(rng, 2), (rows, count), 0, 4096) + boost
    holders = jax.random.permutation(jax.random.fold_in(rng, 3), rows)[jnp.arange(count) % rows]
    tickets = jnp.where(jnp.arange(rows)[:, None] == holders[None, :], 1 << 14, tickets)
    merit = tickets * count + jnp.arange(count)
    return lax.top_k(merit.astype(jnp.int32), top)[1].astype(jnp.int32)


def scatter_about(stream_key, extent, scale, limit, split=(), held_as=jnp.bfloat16):
    entries = scale * jax.random.normal(stream_key, extent, jnp.float32)
    if split:
        entries = entries * block_scale(stream_key, extent, split, -0.22, 0.18)
    return jnp.clip(entries, -limit, limit).astype(held_as)


def setup_inputs(seed: int = 0) -> dict:
    streams_of = jax.random.split(jax.random.key(seed), 8)
    tiles = scatter_about(streams_of[0], (AUX_FNS, ROWS, COLS), 1.0, 6.0, ((0, 8), (1, 4)))
    block_ids = different_ones(streams_of[1], SLABS_ROW * SLABS_AUX, NBLK, NSCR, 0).reshape((SLABS_ROW, SLABS_AUX, NSCR))
    coeffs = scatter_about(streams_of[2], (N, O), COLS ** -0.5, 0.375, ((0, 4),))
    energies = jnp.clip(jax.random.uniform(streams_of[3], (O,), jnp.float32, -1.5, -0.2), -1.5, -0.2)
    tau = jnp.clip(jnp.exp(jax.random.uniform(streams_of[4], (POINTS,), jnp.float32, math.log(0.2), math.log(2.0))), 0.2, 2.0)
    weights = jnp.clip(jnp.exp(jax.random.uniform(streams_of[5], (POINTS,), jnp.float32, math.log(0.3), math.log(1.5))), 0.3, 1.5)
    coupling = scatter_about(streams_of[6], (AUX_FNS, AUX_FNS), AUX_FNS ** -0.5, 0.5)
    return {"tiles": tiles, "block_ids": block_ids, "coeffs": coeffs, "energies": energies, "tau": tau, "weights": weights, "coupling": coupling}


def reference(tiles, block_ids, coeffs, energies, tau, weights, coupling):
    quadrature = jnp.sum(weights[:, None] * jnp.exp(tau[:, None] * energies[None, :]), axis=0)
    offsets = jnp.arange(BLK, dtype=jnp.int32)
    col_index = (block_ids[:, :, :, None] * BLK + offsets).reshape(SLABS_ROW, SLABS_AUX, COLS).astype(jnp.int32)
    coupling_f = coupling.astype(jnp.float32)

    def per_slab(slab_number):
        rows_here = col_index[slab_number]
        picked = jnp.take(coeffs, rows_here.reshape(-1), axis=0).reshape(SLABS_AUX, COLS, O)
        start = (slab_number * ROW_DEV).astype(jnp.int32)
        slab_tiles = lax.dynamic_slice_in_dim(tiles, start, ROW_DEV, 1).reshape(SLABS_AUX, AUX_DEV, ROW_DEV, COLS)
        half_done = jnp.einsum('asmk,aki->masi', slab_tiles.astype(jnp.float32), picked.astype(jnp.float32))
        half_done = lax.optimization_barrier(half_done.astype(jnp.bfloat16)).reshape(ROW_DEV, AUX_FNS, O)
        half_f = half_done.astype(jnp.float32)
        coupled = half_f + jnp.einsum('qp,mpi->mqi', coupling_f, half_f)
        coupled = lax.optimization_barrier(coupled.astype(jnp.bfloat16))
        scaled = lax.optimization_barrier((picked.astype(jnp.float32) * quadrature).astype(jnp.bfloat16))
        grouped = coupled.astype(jnp.float32).reshape(ROW_DEV, SLABS_AUX, AUX_DEV, O)
        gamma_out = jnp.einsum('masi,aki->mask', grouped, scaled.astype(jnp.float32))
        return gamma_out.astype(jnp.bfloat16).reshape(ROW_DEV, AUX_FNS, COLS)

    stacked_out = lax.map(per_slab, jnp.arange(SLABS_ROW, dtype=jnp.int32))
    return stacked_out.reshape(ROWS, AUX_FNS, COLS)
```

```python
import functools
import math

import jax
import jax.numpy as jnp
from jax import lax
from jax.experimental import pallas as pl
from jax.experimental.pallas import tpu as pltpu
from jax.sharding import PartitionSpec as P

BLK = 128
FIRST = 2
SMEM = pl.BlockSpec(memory_space=pltpu.SMEM)
VMEM = pl.BlockSpec(memory_space=pltpu.VMEM)
ANY = pl.BlockSpec(memory_space=pl.ANY)
HBM = pl.BlockSpec(memory_space=pltpu.HBM)


def cost(flops, moved):
    return pl.CostEstimate(flops=flops, bytes_accessed=moved, transcendentals=0)


def swap(array, axis, bit, *after):
    if after:
        array = lax.optimization_barrier((array, *after))[0]
    return lax.ppermute(array, axis, [(i, i ^ bit) for i in range(lax.axis_size(axis))])


def cut_kernel(cuts, tiles_ref, *refs):
    count = len(cuts)
    out_refs, (held_ref, in_sems), to_hbm = refs[:count], refs[count : count + 2], refs[count + 2 :]
    sub = tiles_ref.shape[1] // lax.axis_size("aux")
    here = lax.axis_index("aux")
    copies = []
    for n, (k, first, rows) in enumerate(cuts):
        start = pl.multiple_of((here ^ k) * sub, sub) + first
        source = tiles_ref.at[:, pl.ds(start, rows), :]
        copies.append(pltpu.make_async_copy(source, held_ref.at[n, :, pl.ds(0, rows)], in_sems.at[n]))
        copies[-1].start()
    outs = []
    for n, (_, _, rows) in enumerate(cuts):
        copies[n].wait()
        turned = jnp.swapaxes(held_ref[n, :, :rows], 0, 1)
        if to_hbm:
            to_hbm[0][n, :rows] = turned
            outs.append(pltpu.make_async_copy(to_hbm[0].at[n, pl.ds(0, rows)], out_refs[n], to_hbm[1].at[n]))
            outs[-1].start()
        else:
            out_refs[n][...] = turned
    for copy in outs:
        copy.wait()


def cut_rows(tiles, cuts, to_hbm):
    aux_dev, _, width = tiles.shape
    count, most = len(cuts), max(rows for _, _, rows in cuts)
    scratch = [pltpu.VMEM((count, aux_dev, most, width), tiles.dtype), pltpu.SemaphoreType.DMA((count,))]
    if to_hbm:
        scratch += [pltpu.VMEM((count, most, aux_dev, width), tiles.dtype), pltpu.SemaphoreType.DMA((count,))]
    memory = pltpu.HBM if to_hbm else pltpu.VMEM
    return pl.pallas_call(
        functools.partial(cut_kernel, cuts),
        in_specs=[HBM],
        out_specs=[HBM if to_hbm else VMEM] * count,
        out_shape=[memory((rows, aux_dev, width), tiles.dtype) for _, _, rows in cuts],
        scratch_shapes=scratch,
        name="cut_rows",
        cost_estimate=cost(0, 4 * aux_dev * width * sum(rows for _, _, rows in cuts)),
        compiler_params=pltpu.CompilerParams(vmem_limit_bytes=24 * 2**20),
    )(tiles)


def pick_kernel(owners, ids_ref, energies_ref, tau_ref, weights_ref, *refs):
    held_refs, (picked_ref, scaled_ref, sems) = refs[:-3], refs[-3:]
    slabs, width, _ = picked_ref.shape
    rows = held_refs[0].shape[0]
    unit = math.gcd(rows, BLK)
    fine, per = BLK // unit, rows // unit
    here = lax.axis_index("row")

    def place(b):
        first = pl.multiple_of(b % (width // unit) * unit, unit)
        return picked_ref.at[b // (width // unit), pl.ds(first, unit)]

    def start(b, carry):
        block = b // fine
        piece = ids_ref[0, block % (width // BLK), block // (width // BLK)] * fine + b % fine
        first = pl.multiple_of(piece % per * unit, unit)
        for owner, held_ref in zip(owners, held_refs):
            @pl.when(piece // per == here ^ owner)
            def _():
                pltpu.make_async_copy(held_ref.at[pl.ds(first, unit)], place(b), sems.at[b]).start()
        return carry

    def end(b, carry):
        pltpu.make_async_copy(held_refs[0].at[pl.ds(0, unit)], place(b), sems.at[b]).wait()
        return carry

    lax.fori_loop(0, sems.shape[0], start, 0)
    lax.fori_loop(0, sems.shape[0], end, 0)
    quadrature = sum(weights_ref[t] * jnp.exp(tau_ref[t] * energies_ref[...]) for t in range(tau_ref.shape[0]))
    for a in range(slabs):
        block = picked_ref[a].astype(jnp.float32) * quadrature
        scaled_ref[a] = block.astype(jnp.bfloat16).T


def pick(held, owners, block_ids, energies, tau, weights):
    _, slabs, kept = block_ids.shape
    width, (rows, occ) = kept * BLK, held[0].shape
    return pl.pallas_call(
        functools.partial(pick_kernel, owners),
        in_specs=[SMEM, VMEM, SMEM, SMEM] + [ANY] * len(held),
        out_specs=[VMEM] * 2,
        out_shape=[
            jax.ShapeDtypeStruct((slabs, width, occ), jnp.bfloat16),
            jax.ShapeDtypeStruct((slabs, occ, width), jnp.bfloat16),
        ],
        scratch_shapes=[pltpu.SemaphoreType.DMA((slabs * width // math.gcd(rows, BLK),))],
        name="pick_and_scale",
        cost_estimate=cost(slabs * width * occ, 6 * slabs * width * occ),
        compiler_params=pltpu.CompilerParams(vmem_limit_bytes=24 * 2**20),
    )(jnp.swapaxes(block_ids, 1, 2), energies[None], tau, weights, *held)


def gamma_kernel(first, parts_first, slabs, *refs):
    parts, (picked_ref, scaled_ref, coupling_ref) = refs[:slabs], refs[slabs : slabs + 3]
    out_ref, half_ref, coupled_ref, gamma_ref, sems = refs[-5:]
    rows = half_ref.shape[0]
    _, aux_dev, width = parts[0].shape
    occ = picked_ref.shape[2]
    here = lax.axis_index("aux")
    for k, part in enumerate(parts):
        own = here ^ k
        mine = part[parts_first[k] : parts_first[k] + rows].reshape(rows * aux_dev, width)
        half = jnp.dot(mine, picked_ref[own], preferred_element_type=jnp.float32)
        half = half.astype(jnp.bfloat16).reshape(rows, aux_dev, occ)
        half_ref[:, pl.ds(pl.multiple_of(own * aux_dev, aux_dev), aux_dev), :] = half
    for m in range(rows):
        half = half_ref[m]
        term = jnp.dot(coupling_ref[...], half, preferred_element_type=jnp.float32)
        coupled_ref[m] = (half.astype(jnp.float32) + term).astype(jnp.bfloat16)
    copies = []
    for a in range(slabs):
        fns = pl.ds(a * aux_dev, aux_dev)
        gamma = jnp.dot(
            coupled_ref[:, fns, :].reshape(rows * aux_dev, occ), scaled_ref[a], preferred_element_type=jnp.float32
        )
        gamma_ref[:, fns, :] = gamma.astype(jnp.bfloat16).reshape(rows, aux_dev, width)
        target = out_ref.at[pl.ds(first, rows), fns, :]
        copies.append(pltpu.make_async_copy(gamma_ref.at[:, fns, :], target, sems.at[a]))
        copies[-1].start()
    for copy in copies:
        copy.wait()


def gamma_rows(first, rows, sub, parts, parts_first, picked, scaled, coupling, filled=None):
    slabs, width, occ = picked.shape
    aux_dev = parts[0].shape[1]
    fns = slabs * aux_dev
    operands = [*parts, picked, scaled, coupling]
    in_specs = [VMEM] * len(operands)
    aliases = {}
    if filled is not None:
        aliases = {len(operands): 0}
        operands.append(filled)
        in_specs.append(HBM)
    return pl.pallas_call(
        functools.partial(gamma_kernel, first, parts_first, slabs),
        in_specs=in_specs,
        out_specs=HBM,
        scratch_shapes=[
            pltpu.VMEM((rows, fns, occ), jnp.bfloat16),
            pltpu.VMEM((rows, fns, occ), jnp.bfloat16),
            pltpu.VMEM((rows, fns, width), jnp.bfloat16),
            pltpu.SemaphoreType.DMA((slabs,)),
        ],
        out_shape=jax.ShapeDtypeStruct((sub, fns, width), jnp.bfloat16),
        input_output_aliases=aliases,
        name="gamma_rows",
        cost_estimate=cost(2 * rows * fns * occ * (2 * width + fns), 8 * rows * fns * width + 2**21),
        compiler_params=pltpu.CompilerParams(vmem_limit_bytes=32 * 2**20),
    )(*operands)


def shards(tiles, block_ids, coeffs, energies, tau, weights, coupling):
    slabs = lax.axis_size("aux")
    sub = tiles.shape[1] // slabs
    far = slabs // 2
    cut = sub // 2
    chunks = ((0, cut), (cut, sub - cut))

    long = [(k, 0, sub) for k in range(far, slabs - 1)] + [(slabs - 1, *chunk) for chunk in chunks]
    short = [(k, 0, sub) for k in range(far - 1, -1, -1)]
    tiles = pltpu.with_memory_space_constraint(tiles, pltpu.HBM)
    pieces = cut_rows(tiles, long[:FIRST], False)
    *pieces, tiles, coeffs = lax.optimization_barrier((*pieces, tiles, coeffs))
    owners = range(lax.axis_size("row"))
    held = [swap(coeffs, "row", o) if o else coeffs for o in owners]
    tiles, _ = lax.optimization_barrier((tiles, held[1]))
    tiles = pltpu.with_memory_space_constraint(tiles, pltpu.HBM)
    pieces += cut_rows(tiles, long[FIRST:] + short, True)
    picked, scaled = pick(held, owners, block_ids, energies, tau, weights)

    parts = {short[-1]: pieces[-1]}
    for n, which in enumerate(short[:-1]):
        after = [] if n == 0 else [held[2]] if n == far - 2 else [parts[short[n - 1]]]
        parts[which] = swap(pieces[len(long) + n], "aux", which[0], *after)
    for n, which in enumerate(long):
        after = [parts[long[n - 2]]] if n >= 2 else []
        if n == len(long) - 1:
            after += [parts[long[n - 1]], picked]
        parts[which] = swap(pieces[n], "aux", which[0], *after)

    out = None
    for first, rows in chunks:
        which = [(k, first, rows) if k == slabs - 1 else (k, 0, sub) for k in range(slabs)]
        firsts = [0 if k == slabs - 1 else first for k in range(slabs)]
        out = gamma_rows(first, rows, sub, [parts[w] for w in which], firsts, picked, scaled, coupling, out)
    return out


def solution(mesh):
    in_specs = (P("aux", "row", None), P("row", None, None), P("row", None), P(), P(), P(), P())
    out_specs = P(("row", "aux"), None, None)
    return jax.shard_map(shards, mesh=mesh, in_specs=in_specs, out_specs=out_specs, check_vma=False)
```

```python
import functools
import math

import jax
import jax.numpy as jnp
from jax import lax
from jax.experimental import pallas as pl
from jax.experimental.pallas import tpu as pltpu
from jax.sharding import PartitionSpec as P

BLK = 128
SMEM = pl.BlockSpec(memory_space=pltpu.SMEM)
VMEM = pl.BlockSpec(memory_space=pltpu.VMEM)
ANY = pl.BlockSpec(memory_space=pl.ANY)
HBM = pl.BlockSpec(memory_space=pltpu.HBM)


def cost(flops, moved):
    return pl.CostEstimate(flops=flops, bytes_accessed=moved, transcendentals=0)


def params(mib):
    return pltpu.CompilerParams(vmem_limit_bytes=mib * 2**20)


def swap(array, axis, bit, *after):
    if after:
        array = lax.optimization_barrier((array, *after))[0]
    return lax.ppermute(array, axis, [(i, i ^ bit) for i in range(lax.axis_size(axis))])


def partner_rows(tiles_ref, k, first, rows):
    sub = tiles_ref.shape[1] // lax.axis_size("aux")
    start = pl.multiple_of((lax.axis_index("aux") ^ k) * sub, sub) + first
    return tiles_ref.at[:, pl.ds(start, rows), :]


def slice_kernel(ways, tiles_ref, out_ref, sems):
    copies = []
    for n, k in enumerate(ways):
        source = partner_rows(tiles_ref, k, 0, out_ref.shape[2])
        copies.append(pltpu.make_async_copy(source, out_ref.at[n], sems.at[n]))
        copies[-1].start()
    for copy in copies:
        copy.wait()


def slice_rows(tiles, ways, sub):
    aux_dev, _, width = tiles.shape
    shape = (len(ways), aux_dev, sub, width)
    return pl.pallas_call(
        functools.partial(slice_kernel, ways),
        in_specs=[HBM],
        out_specs=VMEM,
        out_shape=pltpu.VMEM(shape, tiles.dtype),
        scratch_shapes=[pltpu.SemaphoreType.DMA((len(ways),))],
        name="slice_rows",
        cost_estimate=cost(0, 4 * math.prod(shape)),
        compiler_params=params(4),
    )(tiles)


def turn_kernel(both_ref, *out_refs):
    for n, out_ref in enumerate(out_refs):
        out_ref[...] = jnp.swapaxes(both_ref[n], 0, 1)


def turn(both):
    count, aux_dev, sub, width = both.shape
    return pl.pallas_call(
        turn_kernel,
        in_specs=[VMEM],
        out_specs=[VMEM] * count,
        out_shape=[pltpu.VMEM((sub, aux_dev, width), both.dtype)] * count,
        name="turn",
        cost_estimate=cost(0, 4 * both.size),
        compiler_params=params(8),
    )(both)


def cut_kernel(cuts, tiles_ref, *refs):
    count = len(cuts)
    out_refs, (held_ref, turned_ref, in_sems, out_sems) = refs[:count], refs[count:]
    copies = []
    for n, (k, first, rows) in enumerate(cuts):
        source = partner_rows(tiles_ref, k, first, rows)
        copies.append(pltpu.make_async_copy(source, held_ref.at[n, :, pl.ds(0, rows)], in_sems.at[n]))
        copies[-1].start()
    outs = []
    for n, (_, _, rows) in enumerate(cuts):
        copies[n].wait()
        turned_ref[n, :rows] = jnp.swapaxes(held_ref[n, :, :rows], 0, 1)
        outs.append(pltpu.make_async_copy(turned_ref.at[n, pl.ds(0, rows)], out_refs[n], out_sems.at[n]))
        outs[-1].start()
    for copy in outs:
        copy.wait()


def cut_rows(tiles, cuts):
    aux_dev, _, width = tiles.shape
    count, most = len(cuts), max(rows for _, _, rows in cuts)
    return pl.pallas_call(
        functools.partial(cut_kernel, cuts),
        in_specs=[HBM],
        out_specs=[HBM] * count,
        out_shape=[pltpu.HBM((rows, aux_dev, width), tiles.dtype) for _, _, rows in cuts],
        scratch_shapes=[
            pltpu.VMEM((count, aux_dev, most, width), tiles.dtype),
            pltpu.VMEM((count, most, aux_dev, width), tiles.dtype),
            pltpu.SemaphoreType.DMA((count,)),
            pltpu.SemaphoreType.DMA((count,)),
        ],
        name="cut_rows",
        cost_estimate=cost(0, 4 * aux_dev * width * sum(rows for _, _, rows in cuts)),
        compiler_params=params(24),
    )(tiles)


def pick_kernel(owners, ids_ref, energies_ref, tau_ref, weights_ref, *refs):
    held_refs, (picked_ref, scaled_ref, sems) = refs[:-3], refs[-3:]
    slabs, width, _ = picked_ref.shape
    rows = held_refs[0].shape[0]
    unit = math.gcd(rows, BLK)
    fine, per = BLK // unit, rows // unit
    here = lax.axis_index("row")

    def place(b):
        first = pl.multiple_of(b % (width // unit) * unit, unit)
        return picked_ref.at[b // (width // unit), pl.ds(first, unit)]

    def start(b, carry):
        block = b // fine
        piece = ids_ref[0, block % (width // BLK), block // (width // BLK)] * fine + b % fine
        first = pl.multiple_of(piece % per * unit, unit)
        for owner, held_ref in zip(owners, held_refs):
            @pl.when(piece // per == here ^ owner)
            def _():
                pltpu.make_async_copy(held_ref.at[pl.ds(first, unit)], place(b), sems.at[b]).start()
        return carry

    def end(b, carry):
        pltpu.make_async_copy(held_refs[0].at[pl.ds(0, unit)], place(b), sems.at[b]).wait()
        return carry

    lax.fori_loop(0, sems.shape[0], start, 0)
    lax.fori_loop(0, sems.shape[0], end, 0)
    quadrature = sum(weights_ref[t] * jnp.exp(tau_ref[t] * energies_ref[...]) for t in range(tau_ref.shape[0]))
    for a in range(slabs):
        block = picked_ref[a].astype(jnp.float32) * quadrature
        scaled_ref[a] = block.astype(jnp.bfloat16).T


def pick(held, owners, block_ids, energies, tau, weights):
    _, slabs, kept = block_ids.shape
    width, (rows, occ) = kept * BLK, held[0].shape
    return pl.pallas_call(
        functools.partial(pick_kernel, owners),
        in_specs=[SMEM, VMEM, SMEM, SMEM] + [ANY] * len(held),
        out_specs=[VMEM] * 2,
        out_shape=[
            jax.ShapeDtypeStruct((slabs, width, occ), jnp.bfloat16),
            jax.ShapeDtypeStruct((slabs, occ, width), jnp.bfloat16),
        ],
        scratch_shapes=[pltpu.SemaphoreType.DMA((slabs * width // math.gcd(rows, BLK),))],
        name="pick_and_scale",
        cost_estimate=cost(slabs * width * occ, 6 * slabs * width * occ),
        compiler_params=params(24),
    )(jnp.swapaxes(block_ids, 1, 2), energies[None], tau, weights, *held)


def put_half(part, k, picked_ref, half_ref, first):
    rows, aux_dev, width = part.shape
    own = lax.axis_index("aux") ^ k
    half = jnp.dot(part.reshape(rows * aux_dev, width), picked_ref[own], preferred_element_type=jnp.float32)
    half = half.astype(jnp.bfloat16).reshape(rows, aux_dev, half.shape[-1])
    half_ref[first : first + rows, pl.ds(pl.multiple_of(own * aux_dev, aux_dev), aux_dev), :] = half


def half_kernel(*refs):
    for k, part_ref in enumerate(refs[:-2]):
        put_half(part_ref[...], k, refs[-2], refs[-1], 0)


def half_rows(parts, picked):
    slabs, width, occ = picked.shape
    rows, aux_dev, _ = parts[0].shape
    return pl.pallas_call(
        half_kernel,
        in_specs=[VMEM] * (len(parts) + 1),
        out_specs=VMEM,
        out_shape=pltpu.VMEM((rows, slabs * aux_dev, occ), jnp.bfloat16),
        name="half_rows",
        cost_estimate=cost(2 * len(parts) * rows * aux_dev * width * occ, 4 * len(parts) * rows * aux_dev * width),
        compiler_params=params(16),
    )(*parts, picked)


def gamma_kernel(first, aliased, last_ref, picked_ref, scaled_ref, coupling_ref, *refs):
    half_ref, out_ref, coupled_ref, gamma_ref, sems = refs[aliased:]
    rows, aux_dev, width = last_ref.shape
    slabs, occ, _ = scaled_ref.shape
    put_half(last_ref[...], slabs - 1, picked_ref, half_ref, first)
    for m in range(rows):
        half = half_ref[first + m]
        term = jnp.dot(coupling_ref[...], half, preferred_element_type=jnp.float32)
        coupled_ref[m] = (half.astype(jnp.float32) + term).astype(jnp.bfloat16)
    copies = []
    for a in range(slabs):
        fns = pl.ds(a * aux_dev, aux_dev)
        gamma = jnp.dot(
            coupled_ref[:, fns, :].reshape(rows * aux_dev, occ), scaled_ref[a], preferred_element_type=jnp.float32
        )
        gamma_ref[:, fns, :] = gamma.astype(jnp.bfloat16).reshape(rows, aux_dev, width)
        target = out_ref.at[pl.ds(first, rows), fns, :]
        copies.append(pltpu.make_async_copy(gamma_ref.at[:, fns, :], target, sems.at[a]))
        copies[-1].start()
    for copy in copies:
        copy.wait()


def gamma_rows(first, last, picked, scaled, coupling, half, filled=None):
    rows, aux_dev, width = last.shape
    sub, fns, occ = half.shape
    operands = [last, picked, scaled, coupling, half]
    in_specs, aliases = [VMEM] * 5, {4: 0}
    if filled is not None:
        aliases[len(operands)] = 1
        operands.append(filled)
        in_specs.append(HBM)
    return pl.pallas_call(
        functools.partial(gamma_kernel, first, len(aliases)),
        in_specs=in_specs,
        out_specs=[VMEM, HBM],
        out_shape=[pltpu.VMEM(half.shape, half.dtype), jax.ShapeDtypeStruct((sub, fns, width), jnp.bfloat16)],
        input_output_aliases=aliases,
        scratch_shapes=[
            pltpu.VMEM((rows, fns, occ), jnp.bfloat16),
            pltpu.VMEM((rows, fns, width), jnp.bfloat16),
            pltpu.SemaphoreType.DMA((scaled.shape[0],)),
        ],
        name="gamma_rows",
        cost_estimate=cost(2 * rows * fns * occ * (width + fns), 8 * rows * fns * width + 2**21),
        compiler_params=params(24),
    )(*operands)


def shards(tiles, block_ids, coeffs, energies, tau, weights, coupling):
    slabs = lax.axis_size("aux")
    sub = tiles.shape[1] // slabs
    far, cut = slabs // 2, sub // 2
    other = [(k, 0, sub) for k in range(far + 2, slabs - 1)]
    chunks = [(slabs - 1, 0, cut), (slabs - 1, cut, sub - cut)]
    near = [(k, 0, sub) for k in range(far - 1, -1, -1)]

    both = slice_rows(pltpu.with_memory_space_constraint(tiles, pltpu.HBM), (far, far + 1), sub)
    both, tiles, coeffs = lax.optimization_barrier((both, tiles, coeffs))
    owners = range(lax.axis_size("row"))
    held = [swap(coeffs, "row", o) if o else coeffs for o in owners]
    both = swap(both, "aux", far)
    tiles = lax.optimization_barrier((tiles, held[1]))[0]
    pieces = cut_rows(pltpu.with_memory_space_constraint(tiles, pltpu.HBM), [*other, *chunks, *near])
    pieces = dict(zip([*other, *chunks, *near], pieces))
    picked, scaled = pick(held, owners, block_ids, energies, tau, weights)

    parts = {near[-1]: pieces[near[-1]]}
    for n, which in enumerate(near[:-1]):
        after = [] if n == 0 else [held[2]] if n == 1 else [parts[near[n - 2]]]
        parts[which] = swap(pieces[which], "aux", which[0], *after)
    for n, which in enumerate(other):
        after = [held[1]] if n == 0 else [both] if n == 1 else [parts[other[n - 2]]]
        parts[which] = swap(pieces[which], "aux", which[0], *after)
    kept, passed = turn(both)
    parts[far, 0, sub], parts[far + 1, 0, sub] = kept, swap(passed, "aux", 1)
    early = swap(pieces[chunks[0]], "aux", slabs - 1, both)
    late = swap(pieces[chunks[1]], "aux", slabs - 1, parts[other[-1]], picked, *[parts[which] for which in near[1:-1]])

    half = half_rows([parts[k, 0, sub] for k in range(slabs - 1)], picked)
    half, out = gamma_rows(0, early, picked, scaled, coupling, half)
    return gamma_rows(cut, late, picked, scaled, coupling, half, out)[1]


def solution(mesh):
    in_specs = (P("aux", "row", None), P("row", None, None), P("row", None), P(), P(), P(), P())
    out_specs = P(("row", "aux"), None, None)
    return jax.shard_map(shards, mesh=mesh, in_specs=in_specs, out_specs=out_specs, check_vma=False)
```

```python
import functools
import math

import jax
import jax.numpy as jnp
from jax import lax
from jax.experimental import pallas as pl
from jax.experimental.pallas import tpu as pltpu
from jax.sharding import PartitionSpec as P

BLK = 128
SMEM = pl.BlockSpec(memory_space=pltpu.SMEM)
VMEM = pl.BlockSpec(memory_space=pltpu.VMEM)
ANY = pl.BlockSpec(memory_space=pl.ANY)
HBM = pl.BlockSpec(memory_space=pltpu.HBM)


def cost(flops, moved):
    return pl.CostEstimate(flops=flops, bytes_accessed=moved, transcendentals=0)


def params(mib):
    return pltpu.CompilerParams(vmem_limit_bytes=mib * 2**20)


def swap(array, axis, bit, *after):
    if after:
        array = lax.optimization_barrier((array, *after))[0]
    return lax.ppermute(array, axis, [(i, i ^ bit) for i in range(lax.axis_size(axis))])


def partner_rows(tiles_ref, k, first, rows):
    sub = tiles_ref.shape[1] // lax.axis_size("aux")
    start = pl.multiple_of((lax.axis_index("aux") ^ k) * sub, sub) + first
    return tiles_ref.at[:, pl.ds(start, rows), :]


def slice_kernel(ways, tiles_ref, out_ref, sems):
    copies = []
    for n, k in enumerate(ways):
        source = partner_rows(tiles_ref, k, 0, out_ref.shape[2])
        copies.append(pltpu.make_async_copy(source, out_ref.at[n], sems.at[n]))
        copies[-1].start()
    for copy in copies:
        copy.wait()


def slice_rows(tiles, ways, sub):
    aux_dev, _, width = tiles.shape
    shape = (len(ways), aux_dev, sub, width)
    return pl.pallas_call(
        functools.partial(slice_kernel, ways),
        in_specs=[HBM],
        out_specs=VMEM,
        out_shape=pltpu.VMEM(shape, tiles.dtype),
        scratch_shapes=[pltpu.SemaphoreType.DMA((len(ways),))],
        name="slice_rows",
        cost_estimate=cost(0, 4 * math.prod(shape)),
        compiler_params=params(4),
    )(tiles)


def turn_kernel(both_ref, *out_refs):
    for n, out_ref in enumerate(out_refs):
        out_ref[...] = jnp.swapaxes(both_ref[n], 0, 1)


def turn(both):
    count, aux_dev, sub, width = both.shape
    return pl.pallas_call(
        turn_kernel,
        in_specs=[VMEM],
        out_specs=[VMEM] * count,
        out_shape=[pltpu.VMEM((sub, aux_dev, width), both.dtype)] * count,
        name="turn",
        cost_estimate=cost(0, 4 * both.size),
        compiler_params=params(8),
    )(both)


def cut_kernel(cuts, tiles_ref, *refs):
    count = len(cuts)
    out_refs, (held_ref, turned_ref, in_sems, out_sems) = refs[:count], refs[count:]
    copies = []
    for n, (k, first, rows) in enumerate(cuts):
        source = partner_rows(tiles_ref, k, first, rows)
        copies.append(pltpu.make_async_copy(source, held_ref.at[n, :, pl.ds(0, rows)], in_sems.at[n]))
        copies[-1].start()
    outs = []
    for n, (_, _, rows) in enumerate(cuts):
        copies[n].wait()
        turned_ref[n, :rows] = jnp.swapaxes(held_ref[n, :, :rows], 0, 1)
        outs.append(pltpu.make_async_copy(turned_ref.at[n, pl.ds(0, rows)], out_refs[n], out_sems.at[n]))
        outs[-1].start()
    for copy in outs:
        copy.wait()


def cut_rows(tiles, cuts):
    aux_dev, _, width = tiles.shape
    count, most = len(cuts), max(rows for _, _, rows in cuts)
    return pl.pallas_call(
        functools.partial(cut_kernel, cuts),
        in_specs=[HBM],
        out_specs=[HBM] * count,
        out_shape=[pltpu.HBM((rows, aux_dev, width), tiles.dtype) for _, _, rows in cuts],
        scratch_shapes=[
            pltpu.VMEM((count, aux_dev, most, width), tiles.dtype),
            pltpu.VMEM((count, most, aux_dev, width), tiles.dtype),
            pltpu.SemaphoreType.DMA((count,)),
            pltpu.SemaphoreType.DMA((count,)),
        ],
        name="cut_rows",
        cost_estimate=cost(0, 4 * aux_dev * width * sum(rows for _, _, rows in cuts)),
        compiler_params=params(24),
    )(tiles)


def pick_kernel(owners, ids_ref, energies_ref, tau_ref, weights_ref, *refs):
    held_refs, (picked_ref, scaled_ref, sems) = refs[:-3], refs[-3:]
    slabs, width, _ = picked_ref.shape
    rows = held_refs[0].shape[0]
    unit = math.gcd(rows, BLK)
    fine, per = BLK // unit, rows // unit
    here = lax.axis_index("row")

    def place(b):
        first = pl.multiple_of(b % (width // unit) * unit, unit)
        return picked_ref.at[b // (width // unit), pl.ds(first, unit)]

    def start(b, carry):
        block = b // fine
        piece = ids_ref[0, block % (width // BLK), block // (width // BLK)] * fine + b % fine
        first = pl.multiple_of(piece % per * unit, unit)
        for owner, held_ref in zip(owners, held_refs):
            @pl.when(piece // per == here ^ owner)
            def _():
                pltpu.make_async_copy(held_ref.at[pl.ds(first, unit)], place(b), sems.at[b]).start()
        return carry

    def end(b, carry):
        pltpu.make_async_copy(held_refs[0].at[pl.ds(0, unit)], place(b), sems.at[b]).wait()
        return carry

    lax.fori_loop(0, sems.shape[0], start, 0)
    lax.fori_loop(0, sems.shape[0], end, 0)
    quadrature = sum(weights_ref[t] * jnp.exp(tau_ref[t] * energies_ref[...]) for t in range(tau_ref.shape[0]))
    for a in range(slabs):
        block = picked_ref[a].astype(jnp.float32) * quadrature
        scaled_ref[a] = block.astype(jnp.bfloat16).T


def pick(held, owners, block_ids, energies, tau, weights):
    _, slabs, kept = block_ids.shape
    width, (rows, occ) = kept * BLK, held[0].shape
    return pl.pallas_call(
        functools.partial(pick_kernel, owners),
        in_specs=[SMEM, VMEM, SMEM, SMEM] + [ANY] * len(held),
        out_specs=[VMEM] * 2,
        out_shape=[
            jax.ShapeDtypeStruct((slabs, width, occ), jnp.bfloat16),
            jax.ShapeDtypeStruct((slabs, occ, width), jnp.bfloat16),
        ],
        scratch_shapes=[pltpu.SemaphoreType.DMA((slabs * width // math.gcd(rows, BLK),))],
        name="pick_and_scale",
        cost_estimate=cost(slabs * width * occ, 6 * slabs * width * occ),
        compiler_params=params(24),
    )(jnp.swapaxes(block_ids, 1, 2), energies[None], tau, weights, *held)


def put_half(part, k, picked_ref, half_ref, first):
    rows, aux_dev, width = part.shape
    own = lax.axis_index("aux") ^ k
    half = jnp.dot(part.reshape(rows * aux_dev, width), picked_ref[own], preferred_element_type=jnp.float32)
    half = half.astype(jnp.bfloat16).reshape(rows, aux_dev, half.shape[-1])
    half_ref[first : first + rows, pl.ds(pl.multiple_of(own * aux_dev, aux_dev), aux_dev), :] = half


def half_kernel(*refs):
    for k, part_ref in enumerate(refs[:-2]):
        put_half(part_ref[...], k, refs[-2], refs[-1], 0)


def half_rows(parts, picked):
    slabs, width, occ = picked.shape
    rows, aux_dev, _ = parts[0].shape
    return pl.pallas_call(
        half_kernel,
        in_specs=[VMEM] * (len(parts) + 1),
        out_specs=VMEM,
        out_shape=pltpu.VMEM((rows, slabs * aux_dev, occ), jnp.bfloat16),
        name="half_rows",
        cost_estimate=cost(2 * len(parts) * rows * aux_dev * width * occ, 4 * len(parts) * rows * aux_dev * width),
        compiler_params=params(16),
    )(*parts, picked)


def gamma_kernel(first, aliased, last_ref, picked_ref, scaled_ref, coupling_ref, *refs):
    half_ref, out_ref, coupled_ref, gamma_ref, sems = refs[aliased:]
    rows, aux_dev, width = last_ref.shape
    slabs, occ, _ = scaled_ref.shape
    put_half(last_ref[...], slabs - 1, picked_ref, half_ref, first)
    for m in range(rows):
        half = half_ref[first + m]
        term = jnp.dot(coupling_ref[...], half, preferred_element_type=jnp.float32)
        coupled_ref[m] = (half.astype(jnp.float32) + term).astype(jnp.bfloat16)
    copies = []
    for a in range(slabs):
        fns = pl.ds(a * aux_dev, aux_dev)
        gamma = jnp.dot(
            coupled_ref[:, fns, :].reshape(rows * aux_dev, occ), scaled_ref[a], preferred_element_type=jnp.float32
        )
        gamma_ref[:, fns, :] = gamma.astype(jnp.bfloat16).reshape(rows, aux_dev, width)
        target = out_ref.at[pl.ds(first, rows), fns, :]
        copies.append(pltpu.make_async_copy(gamma_ref.at[:, fns, :], target, sems.at[a]))
        copies[-1].start()
    for copy in copies:
        copy.wait()


def gamma_rows(first, last, picked, scaled, coupling, half, filled=None):
    rows, aux_dev, width = last.shape
    sub, fns, occ = half.shape
    operands = [last, picked, scaled, coupling, half]
    in_specs, aliases = [VMEM] * 5, {4: 0}
    if filled is not None:
        aliases[len(operands)] = 1
        operands.append(filled)
        in_specs.append(HBM)
    return pl.pallas_call(
        functools.partial(gamma_kernel, first, len(aliases)),
        in_specs=in_specs,
        out_specs=[VMEM, HBM],
        out_shape=[pltpu.VMEM(half.shape, half.dtype), jax.ShapeDtypeStruct((sub, fns, width), jnp.bfloat16)],
        input_output_aliases=aliases,
        scratch_shapes=[
            pltpu.VMEM((rows, fns, occ), jnp.bfloat16),
            pltpu.VMEM((rows, fns, width), jnp.bfloat16),
            pltpu.SemaphoreType.DMA((scaled.shape[0],)),
        ],
        name="gamma_rows",
        cost_estimate=cost(2 * rows * fns * occ * (width + fns), 8 * rows * fns * width + 2**21),
        compiler_params=params(24),
    )(*operands)


def shards(tiles, block_ids, coeffs, energies, tau, weights, coupling):
    slabs = lax.axis_size("aux")
    sub = tiles.shape[1] // slabs
    far, cut = slabs // 2, sub // 2
    other = [(k, 0, sub) for k in range(far + 2, slabs - 1)]
    chunks = [(slabs - 1, 0, cut), (slabs - 1, cut, sub - cut)]
    near = [(k, 0, sub) for k in range(far - 1, -1, -1)]

    both = slice_rows(pltpu.with_memory_space_constraint(tiles, pltpu.HBM), (far, far + 1), sub)
    both, tiles, coeffs = lax.optimization_barrier((both, tiles, coeffs))
    owners = range(lax.axis_size("row"))
    held = [swap(coeffs, "row", o) if o else coeffs for o in owners]
    both = swap(both, "aux", far)
    pieces = cut_rows(pltpu.with_memory_space_constraint(tiles, pltpu.HBM), [*other, *chunks, *near])
    pieces = dict(zip([*other, *chunks, *near], pieces))
    picked, scaled = pick(held, owners, block_ids, energies, tau, weights)

    parts = {near[-1]: pieces[near[-1]]}
    for n, which in enumerate(near[:-1]):
        after = [] if n == 0 else [parts[near[n - 1]]] if n < len(near) - 2 else [held[1]]
        parts[which] = swap(pieces[which], "aux", which[0], *after)
    for n, which in enumerate(other):
        after = [parts[near[-2]]] if n == 0 else [both] if n == 1 else [parts[other[n - 2]]]
        parts[which] = swap(pieces[which], "aux", which[0], *after)
    kept, passed = turn(both)
    parts[far, 0, sub], parts[far + 1, 0, sub] = kept, swap(passed, "aux", 1)
    early = swap(pieces[chunks[0]], "aux", slabs - 1, both)
    late = swap(pieces[chunks[1]], "aux", slabs - 1, parts[other[-1]], picked)

    half = half_rows([parts[k, 0, sub] for k in range(slabs - 1)], picked)
    half, out = gamma_rows(0, early, picked, scaled, coupling, half)
    return gamma_rows(cut, late, picked, scaled, coupling, half, out)[1]


def solution(mesh):
    in_specs = (P("aux", "row", None), P("row", None, None), P("row", None), P(), P(), P(), P())
    out_specs = P(("row", "aux"), None, None)
    return jax.shard_map(shards, mesh=mesh, in_specs=in_specs, out_specs=out_specs, check_vma=False)
```

```python
import functools
import math

import jax
import jax.numpy as jnp
from jax import lax
from jax.experimental import pallas as pl
from jax.experimental.pallas import tpu as pltpu
from jax.sharding import PartitionSpec as P

BLK = 128
SMEM = pl.BlockSpec(memory_space=pltpu.SMEM)
VMEM = pl.BlockSpec(memory_space=pltpu.VMEM)
ANY = pl.BlockSpec(memory_space=pl.ANY)
HBM = pl.BlockSpec(memory_space=pltpu.HBM)


def cost(flops, moved):
    return pl.CostEstimate(flops=flops, bytes_accessed=moved, transcendentals=0)


def params(mib):
    return pltpu.CompilerParams(vmem_limit_bytes=mib * 2**20)


def swap(array, axis, bit, *after):
    if after:
        array = lax.optimization_barrier((array, *after))[0]
    return lax.ppermute(array, axis, [(i, i ^ bit) for i in range(lax.axis_size(axis))])


def partner_rows(tiles_ref, k, first, rows):
    sub = tiles_ref.shape[1] // lax.axis_size("aux")
    start = pl.multiple_of((lax.axis_index("aux") ^ k) * sub, sub) + first
    return tiles_ref.at[:, pl.ds(start, rows), :]


def slice_kernel(ways, tiles_ref, out_ref, sems):
    copies = []
    for n, k in enumerate(ways):
        source = partner_rows(tiles_ref, k, 0, out_ref.shape[2])
        copies.append(pltpu.make_async_copy(source, out_ref.at[n], sems.at[n]))
        copies[-1].start()
    for copy in copies:
        copy.wait()


def slice_rows(tiles, ways, sub):
    aux_dev, _, width = tiles.shape
    shape = (len(ways), aux_dev, sub, width)
    return pl.pallas_call(
        functools.partial(slice_kernel, ways),
        in_specs=[HBM],
        out_specs=VMEM,
        out_shape=pltpu.VMEM(shape, tiles.dtype),
        scratch_shapes=[pltpu.SemaphoreType.DMA((len(ways),))],
        name="slice_rows",
        cost_estimate=cost(0, 4 * math.prod(shape)),
        compiler_params=params(4),
    )(tiles)


def turn_kernel(both_ref, *out_refs):
    for n, out_ref in enumerate(out_refs):
        out_ref[...] = jnp.swapaxes(both_ref[n], 0, 1)


def turn(both):
    count, aux_dev, sub, width = both.shape
    return pl.pallas_call(
        turn_kernel,
        in_specs=[VMEM],
        out_specs=[VMEM] * count,
        out_shape=[pltpu.VMEM((sub, aux_dev, width), both.dtype)] * count,
        name="turn",
        cost_estimate=cost(0, 4 * both.size),
        compiler_params=params(8),
    )(both)


def cut_kernel(cuts, tiles_ref, *refs):
    count = len(cuts)
    out_refs, (held_ref, turned_ref, in_sems, out_sems) = refs[:count], refs[count:]
    copies = []
    for n, (k, first, rows) in enumerate(cuts):
        source = partner_rows(tiles_ref, k, first, rows)
        copies.append(pltpu.make_async_copy(source, held_ref.at[n, :, pl.ds(0, rows)], in_sems.at[n]))
        copies[-1].start()
    outs = []
    for n, (_, _, rows) in enumerate(cuts):
        copies[n].wait()
        turned_ref[n, :rows] = jnp.swapaxes(held_ref[n, :, :rows], 0, 1)
        outs.append(pltpu.make_async_copy(turned_ref.at[n, pl.ds(0, rows)], out_refs[n], out_sems.at[n]))
        outs[-1].start()
    for copy in outs:
        copy.wait()


def cut_rows(tiles, cuts):
    aux_dev, _, width = tiles.shape
    count, most = len(cuts), max(rows for _, _, rows in cuts)
    return pl.pallas_call(
        functools.partial(cut_kernel, cuts),
        in_specs=[HBM],
        out_specs=[HBM] * count,
        out_shape=[pltpu.HBM((rows, aux_dev, width), tiles.dtype) for _, _, rows in cuts],
        scratch_shapes=[
            pltpu.VMEM((count, aux_dev, most, width), tiles.dtype),
            pltpu.VMEM((count, most, aux_dev, width), tiles.dtype),
            pltpu.SemaphoreType.DMA((count,)),
            pltpu.SemaphoreType.DMA((count,)),
        ],
        name="cut_rows",
        cost_estimate=cost(0, 4 * aux_dev * width * sum(rows for _, _, rows in cuts)),
        compiler_params=params(24),
    )(tiles)


def pick_kernel(owners, ids_ref, energies_ref, tau_ref, weights_ref, *refs):
    held_refs, (picked_ref, scaled_ref, sems) = refs[:-3], refs[-3:]
    slabs, width, _ = picked_ref.shape
    rows = held_refs[0].shape[0]
    unit = math.gcd(rows, BLK)
    fine, per = BLK // unit, rows // unit
    here = lax.axis_index("row")

    def place(b):
        first = pl.multiple_of(b % (width // unit) * unit, unit)
        return picked_ref.at[b // (width // unit), pl.ds(first, unit)]

    def start(b, carry):
        block = b // fine
        piece = ids_ref[0, block % (width // BLK), block // (width // BLK)] * fine + b % fine
        first = pl.multiple_of(piece % per * unit, unit)
        for owner, held_ref in zip(owners, held_refs):
            @pl.when(piece // per == here ^ owner)
            def _():
                pltpu.make_async_copy(held_ref.at[pl.ds(first, unit)], place(b), sems.at[b]).start()
        return carry

    def end(b, carry):
        pltpu.make_async_copy(held_refs[0].at[pl.ds(0, unit)], place(b), sems.at[b]).wait()
        return carry

    lax.fori_loop(0, sems.shape[0], start, 0)
    lax.fori_loop(0, sems.shape[0], end, 0)
    quadrature = sum(weights_ref[t] * jnp.exp(tau_ref[t] * energies_ref[...]) for t in range(tau_ref.shape[0]))
    for a in range(slabs):
        block = picked_ref[a].astype(jnp.float32) * quadrature
        scaled_ref[a] = block.astype(jnp.bfloat16).T


def pick(held, owners, block_ids, energies, tau, weights):
    _, slabs, kept = block_ids.shape
    width, (rows, occ) = kept * BLK, held[0].shape
    return pl.pallas_call(
        functools.partial(pick_kernel, owners),
        in_specs=[SMEM, VMEM, SMEM, SMEM] + [ANY] * len(held),
        out_specs=[VMEM] * 2,
        out_shape=[
            jax.ShapeDtypeStruct((slabs, width, occ), jnp.bfloat16),
            jax.ShapeDtypeStruct((slabs, occ, width), jnp.bfloat16),
        ],
        scratch_shapes=[pltpu.SemaphoreType.DMA((slabs * width // math.gcd(rows, BLK),))],
        name="pick_and_scale",
        cost_estimate=cost(slabs * width * occ, 6 * slabs * width * occ),
        compiler_params=params(24),
    )(jnp.swapaxes(block_ids, 1, 2), energies[None], tau, weights, *held)


def put_half(part, k, picked_ref, half_ref, first):
    rows, aux_dev, width = part.shape
    own = lax.axis_index("aux") ^ k
    half = jnp.dot(part.reshape(rows * aux_dev, width), picked_ref[own], preferred_element_type=jnp.float32)
    half = half.astype(jnp.bfloat16).reshape(rows, aux_dev, half.shape[-1])
    half_ref[first : first + rows, pl.ds(pl.multiple_of(own * aux_dev, aux_dev), aux_dev), :] = half


def half_kernel(ways, *refs):
    for k, part_ref in zip(ways, refs):
        put_half(part_ref[...], k, refs[-2], refs[-1], 0)


def half_rows(ways, parts, picked):
    slabs, width, occ = picked.shape
    rows, aux_dev, _ = parts[0].shape
    return pl.pallas_call(
        functools.partial(half_kernel, ways),
        in_specs=[VMEM] * (len(parts) + 1),
        out_specs=VMEM,
        out_shape=pltpu.VMEM((rows, slabs * aux_dev, occ), jnp.bfloat16),
        name="half_rows",
        cost_estimate=cost(2 * len(parts) * rows * aux_dev * width * occ, 4 * len(parts) * rows * aux_dev * width),
        compiler_params=params(16),
    )(*parts, picked)


def gamma_kernel(last_way, first, aliased, last_ref, picked_ref, scaled_ref, coupling_ref, *refs):
    half_ref, out_ref, coupled_ref, gamma_ref, sems = refs[aliased:]
    rows, aux_dev, width = last_ref.shape
    slabs, occ, _ = scaled_ref.shape
    put_half(last_ref[...], last_way, picked_ref, half_ref, first)
    for m in range(rows):
        half = half_ref[first + m]
        term = jnp.dot(coupling_ref[...], half, preferred_element_type=jnp.float32)
        coupled_ref[m] = (half.astype(jnp.float32) + term).astype(jnp.bfloat16)
    copies = []
    for a in range(slabs):
        fns = pl.ds(a * aux_dev, aux_dev)
        gamma = jnp.dot(
            coupled_ref[:, fns, :].reshape(rows * aux_dev, occ), scaled_ref[a], preferred_element_type=jnp.float32
        )
        gamma_ref[:, fns, :] = gamma.astype(jnp.bfloat16).reshape(rows, aux_dev, width)
        target = out_ref.at[pl.ds(first, rows), fns, :]
        copies.append(pltpu.make_async_copy(gamma_ref.at[:, fns, :], target, sems.at[a]))
        copies[-1].start()
    for copy in copies:
        copy.wait()


def gamma_rows(last_way, first, last, picked, scaled, coupling, half, filled=None):
    rows, aux_dev, width = last.shape
    sub, fns, occ = half.shape
    operands = [last, picked, scaled, coupling, half]
    in_specs, aliases = [VMEM] * 5, {4: 0}
    if filled is not None:
        aliases[len(operands)] = 1
        operands.append(filled)
        in_specs.append(HBM)
    return pl.pallas_call(
        functools.partial(gamma_kernel, last_way, first, len(aliases)),
        in_specs=in_specs,
        out_specs=[VMEM, HBM],
        out_shape=[pltpu.VMEM(half.shape, half.dtype), jax.ShapeDtypeStruct((sub, fns, width), jnp.bfloat16)],
        input_output_aliases=aliases,
        scratch_shapes=[
            pltpu.VMEM((rows, fns, occ), jnp.bfloat16),
            pltpu.VMEM((rows, fns, width), jnp.bfloat16),
            pltpu.SemaphoreType.DMA((scaled.shape[0],)),
        ],
        name="gamma_rows",
        cost_estimate=cost(2 * rows * fns * occ * (width + fns), 8 * rows * fns * width + 2**21),
        compiler_params=params(24),
    )(*operands)


def shards(tiles, block_ids, coeffs, energies, tau, weights, coupling):
    slabs = lax.axis_size("aux")
    sub = tiles.shape[1] // slabs
    far, cut = slabs // 2, sub // 2
    last = far + 2
    other = [(k, 0, sub) for k in range(last + 1, slabs)]
    chunks = [(last, 0, cut), (last, cut, sub - cut)]
    near = [(k, 0, sub) for k in range(far - 1, -1, -1)]

    both = slice_rows(pltpu.with_memory_space_constraint(tiles, pltpu.HBM), (far, far + 1), sub)
    both, tiles, coeffs = lax.optimization_barrier((both, tiles, coeffs))
    owners = range(lax.axis_size("row"))
    held = [swap(coeffs, "row", o) if o else coeffs for o in owners]
    both = swap(both, "aux", far)
    pieces = cut_rows(pltpu.with_memory_space_constraint(tiles, pltpu.HBM), [*other, *chunks, *near])
    pieces = dict(zip([*other, *chunks, *near], pieces))
    picked, scaled = pick(held, owners, block_ids, energies, tau, weights)

    parts = {near[-1]: pieces[near[-1]]}
    for n, which in enumerate(near[:-1]):
        after = [] if n == 0 else [parts[near[n - 1]]] if n < len(near) - 2 else [held[1]]
        parts[which] = swap(pieces[which], "aux", which[0], *after)
    for n, which in enumerate(other):
        after = [parts[near[-2]]] if n == 0 else [both] if n == 1 else [parts[other[n - 2]]]
        parts[which] = swap(pieces[which], "aux", which[0], *after)
    kept, passed = turn(both)
    parts[far, 0, sub], parts[far + 1, 0, sub] = kept, swap(passed, "aux", 1)
    early = swap(pieces[chunks[0]], "aux", last, both)
    late = swap(pieces[chunks[1]], "aux", last, parts[other[-1]], picked)

    ways = [k for k in range(slabs) if k != last]
    half = half_rows(ways, [parts[k, 0, sub] for k in ways], picked)
    half, out = gamma_rows(last, 0, early, picked, scaled, coupling, half)
    return gamma_rows(last, cut, late, picked, scaled, coupling, half, out)[1]


def solution(mesh):
    in_specs = (P("aux", "row", None), P("row", None, None), P("row", None), P(), P(), P(), P())
    out_specs = P(("row", "aux"), None, None)
    return jax.shard_map(shards, mesh=mesh, in_specs=in_specs, out_specs=out_specs, check_vma=False)
```
